32 devices in a mesh: parts: 2 (over y), dp: 4 (over z), tensor: 4 (over x, core).
Axes of the slice: x: 2, y: 2, z: 4, core: 2. Of those that a mesh axis runs over, the one named last changes fastest.
Arguments:
- queries: bfloat16 [256, 64, 128], P(('parts', 'dp'), 'tensor'), parts along dimension 0, may hold values from -4 to 4
- cache_keys: bfloat16 [256, 8, 128, 128], P(('parts', 'dp'), 'tensor'), parts along dimension 0, may hold values from -8 to 8
- cache_values: bfloat16 [256, 8, 128, 128], P(('parts', 'dp'), 'tensor'), parts along dimension 0, may hold values from -6 to 6
- new_key: bfloat16 [256, 8, 128], P(('parts', 'dp'), 'tensor'), parts along dimension 0, may hold values from -8 to 8
- new_value: bfloat16 [256, 8, 128], P(('parts', 'dp'), 'tensor'), parts along dimension 0, may hold values from -6 to 6
- lengths: int32 [8, 32], P(('parts', 'dp')), parts along dimension 0, may hold values from 1 to 128, 2048 in all within a row
- adapter_ids: int32 [256], P(('parts', 'dp')), parts along dimension 0, may hold values from 0 to 31, as said below
- adapter_home: int32 [64], P('parts'), parts along dimension 0, may hold values from 0 to 31, as said below
- w_out: bfloat16 [8192, 4096], P('tensor'), may hold values from -0.0625 to 0.0625
- factor_a: bfloat16 [32, 64, 8192], P('dp', None, 'tensor'), may hold values from -0.0625 to 0.0625
- up_factor_table: bfloat16 [32, 64, 4096], P('dp', None, 'tensor'), may hold values from -0.75 to 0.75
Outputs:
- projected: bfloat16 [256, 4096], P(('parts', 'dp'), 'tensor'), parts along dimension 0
The draws below stay inside these ranges and needn't reach their ends.
There are 2 independent parts, one for each index of `parts`. The reference program is written for one: setup_inputs(seed, part) draws one part's arguments, and reference() takes and returns one part's arrays. A program takes and returns all parts, laid end to end along the dimension named above; an argument that names none is the same for every part. Nothing has to cross between parts.
Inputs may be any that keep to these rules, and one draw needn't show every extreme that they name: `adapter_ids`: the rows of one group name at most 2 different adapters whose storage positions share the value position // 8; in every group some such value is shared by exactly 2 of them. `adapter_home`: A permutation. `lengths`: the 32 entries of one group (one line of the array) sum to 2048; in every group one row has exactly 128 cached positions.
All inputs are finite; a program needn't handle non-finite values.
Results may differ from the reference program's by a relative error of at most 0.008.
Values may be sent and summed in bfloat16 or wider, within the bound.
A program may use at most 128 MiB of HBM per device.

```python
import math
import jax
import jax.numpy as jnp
import numpy as np
from jax import lax

HEADS = 64
KV_HEADS = 8
HEAD_DIM = 128
OUT_WIDTH = 4096
RANK = 64
ADP_DEV = 8
SLOTS = 2
ROWS = 32
LEN = 128
GROUPS = 4
ROWS_ALL = 128
ADAPTERS = 32
ATT_WIDTH = 8192


def routing(key):
    key = jax.random.fold_in(key, 101)
    key_home, key_first, key_second, key_third, key_shift, key_order, key_pick = jax.random.split(key, 7)
    group_count = ROWS_ALL // ROWS
    home = jax.random.permutation(key_home, ADAPTERS).astype(jnp.int32)
    first = jax.random.randint(key_first, (group_count, ROWS), 0, group_count)
    second = jax.random.randint(key_second, (group_count, ROWS), 0, group_count)
    third = jax.random.randint(key_third, (group_count, ROWS), 0, group_count)
    shift = jax.random.randint(key_shift, (), 0, group_count)
    owner_of = (jnp.minimum(jnp.minimum(first, second), third) + shift) % group_count
    owner_of = owner_of.at[:, 1].set(owner_of[:, 0])
    order_keys = jax.random.randint(key_order, (group_count, group_count, ADP_DEV), 0, 1 << 20) * ADP_DEV + jnp.arange(ADP_DEV)
    order = jnp.argsort(order_keys, axis=-1)[:, :, :SLOTS]
    picks = jax.random.randint(key_pick, (group_count, ROWS), 0, SLOTS)
    picks = picks.at[:, 0].set(0).at[:, 1].set(1)
    local_slot = order[jnp.arange(group_count)[:, None], owner_of, picks]
    storage = owner_of * ADP_DEV + local_slot
    inverse = jnp.argsort(home)
    return (home, inverse[storage].reshape(ROWS_ALL).astype(jnp.int32))


def draw_adapter_home(key, part):
    return routing(key)[0]


def draw_adapter_ids(key, part):
    return routing(key)[1]


def draw_queries(key, part):
    key = jax.random.fold_in(key, 11)
    values = jax.random.truncated_normal(key, -4.0, 4.0, (ROWS_ALL, HEADS, HEAD_DIM), jnp.float32)
    return values.astype(jnp.bfloat16)


def draw_cache_keys(key, part):
    key = jax.random.fold_in(key, 12)
    values = jax.random.truncated_normal(key, -4.0, 4.0, (ROWS_ALL, KV_HEADS, LEN, HEAD_DIM), jnp.float32)
    return values.astype(jnp.bfloat16)


def draw_new_key(key, part):
    key = jax.random.fold_in(key, 13)
    values = jax.random.truncated_normal(key, -4.0, 4.0, (ROWS_ALL, KV_HEADS, HEAD_DIM), jnp.float32)
    return values.astype(jnp.bfloat16)


def block_levels(key, extent, shards, smallest, high):
    loudness, own = 1.0, jax.random.fold_in(key, 6)
    for dim, blocks in shards:
        heights = jnp.exp(jax.random.uniform(jax.random.fold_in(own, dim), (blocks,), jnp.float32, smallest / len(shards), high / len(shards)))
        loudness = loudness * jnp.repeat(heights, extent[dim] // blocks).reshape([-1 if axis == dim else 1 for axis in range(len(extent))])
    return loudness


def length_profile(number_of, total, most, lean):
    weights = [(1 << 20) // math.isqrt(rank ** lean) + 1 for rank in range(2, number_of + 1)]
    rest, counts = total - most - (number_of - 1), [1] * (number_of - 1)
    while rest > 0:
        candidates = [i for i in range(number_of - 1) if counts[i] < most]
        pool, remaining = sum([weights[i] for i in candidates]), rest
        for i in candidates:
            extra = min(most - counts[i], max(1, remaining * weights[i] // pool), rest)
            counts[i] = counts[i] + extra
            rest = rest - extra
    return np.array([most] + counts)


def ragged(rng, number_of, total, reach, lean):
    if number_of == 2:
        one = jax.random.randint(rng, (), max(1, total - reach), min(reach, total - 1) + 1)
        return jnp.stack([one, total - one])
    sizes = jnp.asarray(length_profile(number_of, total, reach, lean), jnp.int32)
    couples = (number_of - 1) // 2
    source_of, sink = sizes[1:1 + 2 * couples:2], sizes[2:2 + 2 * couples:2]
    room = jnp.minimum(source_of - 1, reach - sink)
    moved = jax.random.randint(jax.random.fold_in(rng, 1), (couples,), 0, 1 << 20) % (room + 1)
    sizes = sizes.at[1:1 + 2 * couples:2].set(source_of - moved).at[2:2 + 2 * couples:2].set(sink + moved)
    return sizes[jax.random.permutation(jax.random.fold_in(rng, 2), number_of)]


def normal_values(key, shape, scale, reach, cuts=(), held_as=jnp.bfloat16):
    entries = scale * jax.random.normal(key, shape, jnp.float32)
    if cuts:
        entries = entries * block_levels(key, shape, cuts, -0.22, 0.18)
    return jnp.clip(entries, -reach, reach).astype(held_as)


def setup_inputs(seed: int = 0, part: int = 0) -> dict:
    keys = jax.random.split(jax.random.key(seed), 12)
    own_keys = jax.random.split(jax.random.fold_in(keys[11], part), 12)
    queries = draw_queries(jax.random.fold_in(jax.random.fold_in(keys[11], part), 71), part)
    cache_keys = draw_cache_keys(jax.random.fold_in(jax.random.fold_in(keys[11], part), 71), part)
    cache_values = normal_values(own_keys[2], (ROWS_ALL, KV_HEADS, LEN, HEAD_DIM), 1.0, 6.0, ((0, 4), (1, 4)))
    new_key = draw_new_key(jax.random.fold_in(jax.random.fold_in(keys[11], part), 71), part)
    new_value = normal_values(own_keys[4], (ROWS_ALL, KV_HEADS, HEAD_DIM), 1.0, 6.0, ((0, 4), (1, 4)))
    lengths = jax.vmap(lambda own: ragged(own, ROWS, ROWS * LEN // 2, LEN, 1))(jax.random.split(own_keys[5], GROUPS)).reshape((GROUPS, ROWS)).astype(jnp.int32)
    adapter_ids = draw_adapter_ids(jax.random.fold_in(jax.random.fold_in(keys[11], part), 71), part)
    adapter_home = draw_adapter_home(jax.random.fold_in(jax.random.fold_in(keys[11], part), 71), part)
    w_out = normal_values(keys[8], (ATT_WIDTH, OUT_WIDTH), ATT_WIDTH ** -0.5, 0.0625, ((0, 4),))
    factor_a = normal_values(keys[9], (ADAPTERS, RANK, ATT_WIDTH), ATT_WIDTH ** -0.5, 0.0625, ((0, 4), (2, 4)))
    up_factor_table = normal_values(keys[10], (ADAPTERS, RANK, OUT_WIDTH), RANK ** -0.5, 0.75, ((0, 4), (2, 4)))
    return {"queries": queries, "cache_keys": cache_keys, "cache_values": cache_values, "new_key": new_key, "new_value": new_value, "lengths": lengths, "adapter_ids": adapter_ids, "adapter_home": adapter_home, "w_out": w_out, "factor_a": factor_a, "up_factor_table": up_factor_table}


ADAPTER_SCALING = 2.0

def attend(queries, cache_keys, cache_values, new_key, new_value, lengths):
    row_count, head_count, head_width = queries.shape
    kv_count = cache_keys.shape[1]
    cache_span = cache_keys.shape[2]
    grouped = queries.astype(jnp.float32).reshape(row_count, kv_count, head_count // kv_count, head_width)
    score_scale = 1.0 / math.sqrt(head_width)
    scores = jnp.einsum('rkgd,rkpd->rkgp', grouped, cache_keys.astype(jnp.float32)) * score_scale
    own_score = jnp.einsum('rkgd,rkd->rkg', grouped, new_key.astype(jnp.float32)) * score_scale
    visible = jnp.arange(cache_span)[None, :] < lengths.reshape(row_count)[:, None]
    visible = visible[:, None, None, :]
    row_top = jnp.maximum(lax.optimization_barrier(jnp.max(jnp.where(visible, scores, -jnp.inf), axis=-1)), own_score)
    weights = jnp.where(visible, jnp.exp(scores - row_top[..., None]), 0.0)
    own_weight = jnp.exp(own_score - row_top)
    row_total = lax.optimization_barrier(jnp.sum(weights, axis=-1)) + own_weight
    probs = (weights / row_total[..., None]).astype(jnp.bfloat16)
    own_prob = (own_weight / row_total).astype(jnp.bfloat16)
    mixed = jnp.einsum('rkgp,rkpd->rkgd', probs.astype(jnp.float32), cache_values.astype(jnp.float32))
    mixed = mixed + own_prob.astype(jnp.float32)[..., None] * new_value.astype(jnp.float32)[:, :, None, :]
    return mixed.astype(jnp.bfloat16).reshape(row_count, head_count * head_width)

def reference(queries, cache_keys, cache_values, new_key, new_value, lengths, adapter_ids, adapter_home, w_out, factor_a, up_factor_table):
    attended = attend(queries, cache_keys, cache_values, new_key, new_value, lengths)
    base_output = jnp.dot(attended, w_out, preferred_element_type=jnp.float32)
    position = adapter_home[adapter_ids].astype(jnp.int32)
    shrink_all = jnp.einsum('rj,akj->rak', attended.astype(jnp.float32), factor_a.astype(jnp.float32))
    shrunk = jnp.take_along_axis(shrink_all, position[:, None, None], axis=1)[:, 0, :].astype(jnp.bfloat16)
    adapter_total = factor_a.shape[0]
    adapter_rank_width = factor_a.shape[1]
    chosen = position[:, None] == jnp.arange(adapter_total, dtype=jnp.int32)[None, :]
    slot_block_rows = jnp.where(chosen[:, :, None], shrunk[:, None, :], jnp.zeros((), jnp.bfloat16))
    slot_block_rows = slot_block_rows.reshape(position.shape[0], adapter_total * adapter_rank_width)
    adapter_delta = jnp.dot(slot_block_rows, up_factor_table.reshape(adapter_total * adapter_rank_width, up_factor_table.shape[2]), preferred_element_type=jnp.float32)
    return (base_output + ADAPTER_SCALING * adapter_delta).astype(jnp.bfloat16)
```

```python
import functools
import math

import jax
import jax.numpy as jnp
from jax import lax
from jax.experimental import pallas as pl
from jax.experimental.pallas import tpu as pltpu
from jax.sharding import PartitionSpec as P

ADAPTER_SCALING = 2.0
MESH = pl.DeviceIdType.MESH
F32 = jnp.float32
BF16 = jnp.bfloat16
LANES = 128


def iota(shape, dim):
    return lax.broadcasted_iota(jnp.int32, shape, dim)


def column(row, count, spread):
    shape = (count * spread, count)
    own = iota(shape, 0) // spread == iota(shape, 1)
    return jnp.sum(jnp.where(own, row.astype(F32), 0.0), axis=1, keepdims=True)


def kernel(
    n, nt, rank,
    lengths_ref, ids_ref, home_ref, new_key_ref, new_value_ref,
    queries_hbm, keys_hbm, values_hbm, w_hbm, a_hbm, up_hbm,
    out_ref,
    queries, keys, values, w, a, up,
    mixed_rows, att, positions, shrunk, base_send, base_recv, base_own, delta_send, delta_recv,
    load_q, load_k, load_v, load_w, load_a, load_up,
    pos_send, pos_recv, right_send, right_recv, left_send, left_recv,
    shrink_send, shrink_recv, bsend, brecv, dsend, drecv,
):
    rows, heads, width = queries.shape
    kv = keys.shape[0]
    per_kv = heads // kv
    feats = per_kv * width
    out_share = up.shape[1]
    stored = up.shape[0] // rank
    me = lax.axis_index("dp")
    mt = lax.axis_index("tensor")

    def block(t):
        return pl.ds(pl.multiple_of(t * out_share, out_share), out_share)

    get_q = pltpu.make_async_copy(queries_hbm, queries, load_q)
    get_q.start()
    get_k, get_v = [], []
    for c in range(kv):
        get_k.append(pltpu.make_async_copy(keys_hbm.at[:, c], keys.at[c], load_k.at[c]))
        get_v.append(pltpu.make_async_copy(values_hbm.at[:, c], values.at[c], load_v.at[c]))
        get_k[c].start()
        get_v[c].start()
    get_w = []
    for i in range(nt):
        t = lax.rem(mt + 1 + i, nt)
        get_w.append(pltpu.make_async_copy(w_hbm.at[:, block(t)], w.at[i], load_w.at[i]))
        get_w[i].start()
    get_a = pltpu.make_async_copy(a_hbm, a, load_a)
    get_a.start()
    get_up = pltpu.make_async_copy(up_hbm, up, load_up)
    get_up.start()

    barrier = pltpu.get_barrier_semaphore()
    for i in range(1, n):
        pl.semaphore_signal(barrier, inc=1, device_id={"dp": lax.rem(me + i, n)}, device_id_type=MESH)
    for i in range(1, nt):
        pl.semaphore_signal(barrier, inc=1, device_id={"tensor": lax.rem(mt + i, nt)}, device_id_type=MESH)

    adapters = home_ref.shape[1]
    id_column = column(ids_ref[...], rows, 1)
    match = id_column == iota((rows, adapters), 1).astype(F32)
    position = jnp.sum(jnp.where(match, home_ref[...].astype(F32), 0.0), axis=1, keepdims=True)
    positions[me] = jnp.broadcast_to(position, (rows, LANES))

    count = rows * per_kv
    visible_to = column(lengths_ref[...], rows, per_kv)
    visible = iota((count, keys.shape[2]), 1).astype(F32) < visible_to
    scale = 1.0 / math.sqrt(width)

    def line(c, source, step, to_right):
        send, recv = (right_send, right_recv) if to_right else (left_send, left_recv)
        return pltpu.make_async_remote_copy(
            src_ref=att.at[c, source], dst_ref=att.at[c, source],
            send_sem=send.at[c, step], recv_sem=recv.at[c, step],
            device_id={"dp": me + 1 if to_right else me - 1}, device_id_type=MESH,
        )

    def first_hop(c):
        @pl.when(me < n - 1)
        def _():
            line(c, me, 0, True).start()

        @pl.when(me > 0)
        def _():
            line(c, me, 0, False).start()

    def forward(c, hop):
        @pl.when(me >= hop)
        def _():
            line(c, me - hop, hop - 1, True).wait_recv()

            @pl.when(me < n - 1)
            def _():
                if hop < n - 1:
                    line(c, me - hop, hop, True).start()

        @pl.when(me + hop <= n - 1)
        def _():
            line(c, me + hop, hop - 1, False).wait_recv()

            @pl.when(me > 0)
            def _():
                if hop < n - 1:
                    line(c, me + hop, hop, False).start()

    def pos_copy(i):
        return pltpu.make_async_remote_copy(
            src_ref=positions.at[me], dst_ref=positions.at[me],
            send_sem=pos_send.at[i], recv_sem=pos_recv.at[i],
            device_id={"dp": lax.rem(me + i, n)}, device_id_type=MESH,
        )

    get_q.wait()
    for c in range(kv):
        q = queries[...]
        get_k[c].wait()
        scores = lax.dot_general(
            q, keys[c], (((2,), (2,)), ((0,), (0,))), preferred_element_type=F32
        )[:, c * per_kv:(c + 1) * per_kv, :].reshape(count, keys.shape[2]) * scale
        pick = (iota((count, rows * kv), 1) == (iota((count, rows * kv), 0) // per_kv) * kv + c).astype(BF16)
        own_key = jnp.dot(pick, new_key_ref[...], preferred_element_type=F32)
        own_value = jnp.dot(pick, new_value_ref[...], preferred_element_type=F32)
        qc = q.astype(F32)[:, c * per_kv:(c + 1) * per_kv, :].reshape(count, width)
        own = jnp.sum(qc * own_key, axis=1, keepdims=True) * scale
        top = jnp.maximum(jnp.max(jnp.where(visible, scores, -jnp.inf), axis=1, keepdims=True), own)
        weights = jnp.where(visible, jnp.exp(scores - top), 0.0)
        own_weight = jnp.exp(own - top)
        total = jnp.sum(weights, axis=1, keepdims=True) + own_weight
        probs = (weights / total).reshape(rows, per_kv, keys.shape[2]).astype(BF16)
        own_prob = (own_weight / total).astype(BF16).astype(F32)
        get_v[c].wait()
        mixed = lax.dot_general(
            probs, values[c], (((2,), (1,)), ((0,), (0,))), preferred_element_type=F32
        ).reshape(count, width)
        mixed_rows[...] = mixed + own_prob * own_value
        for g in range(per_kv):
            att[c, me, :, g * width:(g + 1) * width] = mixed_rows[pl.ds(g, rows, stride=per_kv), :].astype(BF16)
        if c == 0:
            pl.semaphore_wait(barrier, n - 1 + nt - 1)
            for i in range(1, n):
                pos_copy(i).start()
        first_hop(c)

    hops = [(c, hop) for hop in range(1, n) for c in range(kv)]
    per_step = -(-len(hops) // nt)

    def base_copy(i):
        return pltpu.make_async_remote_copy(
            src_ref=base_send.at[i], dst_ref=base_recv.at[i],
            send_sem=bsend.at[i], recv_sem=brecv.at[i],
            device_id={"tensor": lax.rem(mt + 1 + i, nt)}, device_id_type=MESH,
        )

    for i in range(nt):
        get_w[i].wait()
        partial = jnp.zeros((rows, out_share), F32)
        for c in range(kv):
            partial = partial + jnp.dot(
                att[c, me], w[i, c * feats:(c + 1) * feats, :], preferred_element_type=F32
            )
        if i < nt - 1:
            base_send[i] = partial.astype(BF16)
            base_copy(i).start()
        else:
            base_own[...] = partial
        for c, hop in hops[i * per_step:(i + 1) * per_step]:
            forward(c, hop)
    get_a.wait()
    for i in range(1, n):
        pos_copy(i).wait_recv()

    every = n * rows
    packs = LANES // rank
    half = iota((every, LANES), 1) // rank
    where = positions[...].reshape(every, LANES) - (me * stored).astype(F32)
    down = jnp.zeros((every, stored * rank), F32)
    for c in range(kv):
        down = down + lax.dot_general(
            att[c].reshape(every, feats), a[:, c * feats:(c + 1) * feats],
            (((1,), (1,)), ((), ())), preferred_element_type=F32,
        )
    folded = jnp.zeros((every, LANES), F32)
    for j in range(stored // packs):
        mine = where == (half + j * packs).astype(F32)
        folded = folded + jnp.where(mine, down[:, j * LANES:(j + 1) * LANES], 0.0)
    folded = folded + pltpu.roll(folded, rank, 1)
    short = every // 2
    low = iota((short, LANES), 1) < rank
    shrunk[0] = jnp.where(low, folded[:short], folded[short:]).astype(BF16)

    def shrink_copy(i):
        return pltpu.make_async_remote_copy(
            src_ref=shrunk.at[0], dst_ref=shrunk.at[i],
            send_sem=shrink_send.at[i], recv_sem=shrink_recv.at[i],
            device_id={"tensor": lax.rem(mt + i, nt)}, device_id_type=MESH,
        )

    for i in range(1, nt):
        shrink_copy(i).start()
    get_up.wait()
    total = shrunk[0].astype(F32)
    for i in range(1, nt):
        shrink_copy(i).wait_recv()
        total = total + shrunk[i].astype(F32)
    turned = pltpu.roll(total, rank, 1)
    whole = jnp.concatenate([jnp.where(low, total, turned), jnp.where(low, turned, total)], axis=0)
    spread = jnp.concatenate(
        [jnp.where(where == (half + j * packs).astype(F32), whole, 0.0) for j in range(stored // packs)], axis=1
    ).astype(BF16)

    delta = jnp.dot(spread, up[...], preferred_element_type=F32) * ADAPTER_SCALING
    delta_send[...] = delta.astype(BF16).reshape(n, rows, out_share)

    def delta_copy(i):
        to = lax.rem(me + i, n)
        return pltpu.make_async_remote_copy(
            src_ref=delta_send.at[to], dst_ref=delta_recv.at[i - 1],
            send_sem=dsend.at[i - 1], recv_sem=drecv.at[i - 1],
            device_id={"dp": to}, device_id_type=MESH,
        )

    for i in range(1, n):
        delta_copy(i).start()
    result = base_own[...] + delta_send[me].astype(F32)
    for i in range(nt - 1):
        base_copy(i).wait_recv()
        result = result + base_recv[i].astype(F32)
    for i in range(1, n):
        delta_copy(i).wait_recv()
        result = result + delta_recv[i - 1].astype(F32)
    out_ref[...] = result.astype(BF16)

    for i in range(1, n):
        pos_copy(i).wait_send()
        delta_copy(i).wait_send()
    for i in range(1, nt):
        shrink_copy(i).wait_send()
    for i in range(nt - 1):
        base_copy(i).wait_send()
    for c in range(kv):
        for step in range(n - 1):
            @pl.when((me < n - 1) & (me >= step))
            def _():
                line(c, me - step, step, True).wait_send()

            @pl.when((me > 0) & (me + step <= n - 1))
            def _():
                line(c, me + step, step, False).wait_send()


def local(
    n, nt,
    queries, cache_keys, cache_values, new_key, new_value, lengths,
    adapter_ids, adapter_home, w_out, factor_a, up_factor_table,
):
    rows, heads, width = queries.shape
    kv, span = cache_keys.shape[1:3]
    stored, rank, feats_all = factor_a.shape
    out_share = up_factor_table.shape[2]
    feats = feats_all // kv
    per_kv = heads // kv
    dma = pltpu.SemaphoreType.DMA
    vmem = pl.BlockSpec(memory_space=pltpu.VMEM)
    hbm = pl.BlockSpec(memory_space=pl.ANY)
    return pl.pallas_call(
        functools.partial(kernel, n, nt, rank),
        out_shape=jax.ShapeDtypeStruct((rows, out_share), BF16),
        in_specs=[vmem] * 5 + [hbm] * 6,
        out_specs=vmem,
        scratch_shapes=[
            pltpu.VMEM((rows, heads, width), BF16),
            pltpu.VMEM((kv, rows, span, width), BF16),
            pltpu.VMEM((kv, rows, span, width), BF16),
            pltpu.VMEM((nt, feats_all, out_share), BF16),
            pltpu.VMEM((stored * rank, feats_all), BF16),
            pltpu.VMEM((stored * rank, out_share), BF16),
            pltpu.VMEM((rows * per_kv, width), F32),
            pltpu.VMEM((kv, n, rows, feats), BF16),
            pltpu.VMEM((n, rows, LANES), F32),
            pltpu.VMEM((nt, n * rows // 2, LANES), BF16),
            pltpu.VMEM((nt - 1, rows, out_share), BF16),
            pltpu.VMEM((nt - 1, rows, out_share), BF16),
            pltpu.VMEM((rows, out_share), F32),
            pltpu.VMEM((n, rows, out_share), BF16),
            pltpu.VMEM((n - 1, rows, out_share), BF16),
            dma, dma((kv,)), dma((kv,)), dma((nt,)), dma, dma,
            dma((n,)), dma((n,)),
            dma((kv, n)), dma((kv, n)), dma((kv, n)), dma((kv, n)),
            dma((nt,)), dma((nt,)),
            dma((nt,)), dma((nt,)),
            dma((n,)), dma((n,)),
        ],
        compiler_params=pltpu.CompilerParams(
            collective_id=0, has_side_effects=True, vmem_limit_bytes=52 * 1024 * 1024
        ),
        name="attend_project",
    )(
        lengths, adapter_ids.reshape(1, rows), adapter_home.reshape(1, -1),
        new_key.reshape(rows * kv, width), new_value.reshape(rows * kv, width),
        queries, cache_keys, cache_values, w_out,
        factor_a.reshape(stored * rank, feats_all), up_factor_table.reshape(stored * rank, out_share),
    )


def solution(mesh):
    in_specs = (
        P(("parts", "dp"), "tensor", None),
        P(("parts", "dp"), "tensor", None, None),
        P(("parts", "dp"), "tensor", None, None),
        P(("parts", "dp"), "tensor", None),
        P(("parts", "dp"), "tensor", None),
        P(("parts", "dp"), None),
        P(("parts", "dp")),
        P("parts"),
        P("tensor", None),
        P("dp", None, "tensor"),
        P("dp", None, "tensor"),
    )
    out_specs = P(("parts", "dp"), "tensor")
    body = functools.partial(local, mesh.shape["dp"], mesh.shape["tensor"])
    return jax.shard_map(body, mesh=mesh, in_specs=in_specs, out_specs=out_specs, check_vma=False)
```

```python
import functools
import math

import jax
import jax.numpy as jnp
from jax import lax
from jax.experimental import pallas as pl
from jax.experimental.pallas import tpu as pltpu
from jax.sharding import PartitionSpec as P

ADAPTER_SCALING = 2.0
MESH = pl.DeviceIdType.MESH
F32 = jnp.float32
BF16 = jnp.bfloat16
LANES = 128
HALVES = 1
GREETED = 0
STRIDES = (1, 1)


def iota(shape, dim):
    return lax.broadcasted_iota(jnp.int32, shape, dim)


def stride(j):
    return STRIDES[min(j, len(STRIDES) - 1)]


def column(row, count, spread):
    shape = (count * spread, count)
    own = iota(shape, 0) // spread == iota(shape, 1)
    return jnp.sum(jnp.where(own, row.astype(F32), 0.0), axis=1, keepdims=True)


def kernel(
    n, nt, rank,
    lengths_hbm, ids_hbm, home_hbm, new_key_hbm, new_value_hbm,
    queries_hbm, keys_hbm, values_hbm, w_hbm, a_hbm, up_hbm,
    out_ref,
    lengths, ids, home, new_key, new_value,
    queries, keys, values, w, a, up,
    mixed_rows, own_att, att, positions, shrunk, base_send, base_recv, base_own, delta_send, delta_recv,
    load_small, load_q, load_k, load_v, load_w, load_a, load_up,
    pos_send, pos_recv, right_send, right_recv, left_send, left_recv,
    shrink_send, shrink_recv, bsend, brecv, dsend, drecv,
):
    rows, heads, width = queries.shape
    kv, span = keys.shape[0], keys.shape[2]
    per_kv = heads // kv
    feats = per_kv * width
    out_share = up.shape[1]
    stored = up.shape[0] // rank
    part = rows // HALVES
    me = lax.axis_index("dp")
    mt = lax.axis_index("tensor")

    def block(t):
        return pl.ds(pl.multiple_of(t * out_share, out_share), out_share)

    small = [(ids_hbm, ids), (home_hbm, home), (lengths_hbm, lengths), (new_key_hbm, new_key), (new_value_hbm, new_value)]
    get_small = [pltpu.make_async_copy(x, y, load_small.at[i]) for i, (x, y) in enumerate(small)]
    for get in get_small:
        get.start()
    get_q = pltpu.make_async_copy(queries_hbm, queries, load_q)
    get_q.start()
    chunks = [(h, k) for h in range(HALVES) for k in range(kv)]
    get_k, get_v = [], []
    for j, (h, k) in enumerate(chunks):
        here = pl.ds(h * part, part)
        get_k.append(pltpu.make_async_copy(keys_hbm.at[here, k], keys.at[k, here], load_k.at[j]))
        get_v.append(pltpu.make_async_copy(values_hbm.at[here, k], values.at[k, here], load_v.at[j]))
        get_k[j].start()
        get_v[j].start()
    get_w = []
    for i in range(nt):
        t = lax.rem(mt + 1 + i, nt)
        get_w.append(pltpu.make_async_copy(w_hbm.at[:, block(t)], w.at[i], load_w.at[i]))
    get_a = pltpu.make_async_copy(a_hbm, a, load_a)
    get_up = pltpu.make_async_copy(up_hbm, up, load_up)

    barrier = pltpu.get_barrier_semaphore()
    for i in range(1, n):
        pl.semaphore_signal(barrier, inc=1, device_id={"dp": lax.rem(me + i, n)}, device_id_type=MESH)
    for i in range(1, nt):
        pl.semaphore_signal(barrier, inc=1, device_id={"tensor": lax.rem(mt + i, nt)}, device_id_type=MESH)

    for get in get_small:
        get.wait()
    adapters = home.shape[1]
    id_column = column(ids[...], rows, 1)
    match = id_column == iota((rows, adapters), 1).astype(F32)
    position = jnp.sum(jnp.where(match, home[...].astype(F32), 0.0), axis=1, keepdims=True)
    positions[me] = jnp.broadcast_to(position, (rows, LANES))

    def line(j, slot, distance, step, sign):
        send, recv = (right_send, right_recv) if sign > 0 else (left_send, left_recv)
        return pltpu.make_async_remote_copy(
            src_ref=att.at[j, slot], dst_ref=att.at[j, slot],
            send_sem=send.at[j, distance], recv_sem=recv.at[j, distance],
            device_id={"dp": me + sign * step}, device_id_type=MESH,
        )

    def reaches(offset):
        return (me + offset >= 0) & (me + offset <= n - 1)

    def pass_on(j, source, act):
        for step in range(min(stride(j), n - 1), 0, -1):
            for sign in (1, -1):
                if source + step < n:
                    @pl.when(reaches(sign * step) & reaches(-sign * source))
                    def _():
                        act(line(j, me - sign * source, source + step, step, sign))

    def arrive(j, distance):
        for sign in (1, -1):
            @pl.when(reaches(-sign * distance))
            def _():
                came = (distance - 1) % stride(j) + 1
                line(j, me - sign * distance, distance, came, sign).wait_recv()
        if distance % stride(j) == 0:
            pass_on(j, distance, lambda copy: copy.start())

    def pos_copy(i):
        return pltpu.make_async_remote_copy(
            src_ref=positions.at[me], dst_ref=positions.at[me],
            send_sem=pos_send.at[i], recv_sem=pos_recv.at[i],
            device_id={"dp": lax.rem(me + i, n)}, device_id_type=MESH,
        )

    def base_copy(i):
        return pltpu.make_async_remote_copy(
            src_ref=base_send.at[i], dst_ref=base_recv.at[i],
            send_sem=bsend.at[i], recv_sem=brecv.at[i],
            device_id={"tensor": lax.rem(mt + 1 + i, nt)}, device_id_type=MESH,
        )

    def shrink_copy(h, i):
        return pltpu.make_async_remote_copy(
            src_ref=shrunk.at[h, 0], dst_ref=shrunk.at[h, i],
            send_sem=shrink_send.at[h, i], recv_sem=shrink_recv.at[h, i],
            device_id={"tensor": lax.rem(mt + i, nt)}, device_id_type=MESH,
        )

    def delta_copy(h, i):
        to = lax.rem(me + i, n)
        return pltpu.make_async_remote_copy(
            src_ref=delta_send.at[h, to], dst_ref=delta_recv.at[h, i - 1],
            send_sem=dsend.at[h, i - 1], recv_sem=drecv.at[h, i - 1],
            device_id={"dp": to}, device_id_type=MESH,
        )

    count = part * per_kv
    scale = 1.0 / math.sqrt(width)
    reach = column(lengths[...], rows, per_kv)
    get_q.wait()
    for j, (h, k) in enumerate(chunks):
        visible = iota((count, span), 1).astype(F32) < reach[h * count:(h + 1) * count]
        q = queries[h * part:(h + 1) * part]
        get_k[j].wait()
        scores = lax.dot_general(
            q, keys[k, h * part:(h + 1) * part], (((2,), (2,)), ((0,), (0,))), preferred_element_type=F32
        )[:, k * per_kv:(k + 1) * per_kv, :].reshape(count, span) * scale
        row = iota((count, rows * kv), 0) // per_kv + h * part
        pick = (iota((count, rows * kv), 1) == row * kv + k).astype(BF16)
        own_key = jnp.dot(pick, new_key[...], preferred_element_type=F32)
        own_value = jnp.dot(pick, new_value[...], preferred_element_type=F32)
        qk = q.astype(F32)[:, k * per_kv:(k + 1) * per_kv, :].reshape(count, width)
        own = jnp.sum(qk * own_key, axis=1, keepdims=True) * scale
        top = jnp.maximum(jnp.max(jnp.where(visible, scores, -jnp.inf), axis=1, keepdims=True), own)
        weights = jnp.where(visible, jnp.exp(scores - top), 0.0)
        own_weight = jnp.exp(own - top)
        total = jnp.sum(weights, axis=1, keepdims=True) + own_weight
        probs = (weights / total).reshape(part, per_kv, span).astype(BF16)
        own_prob = (own_weight / total).astype(BF16).astype(F32)
        get_v[j].wait()
        mixed = lax.dot_general(
            probs, values[k, h * part:(h + 1) * part], (((2,), (1,)), ((0,), (0,))), preferred_element_type=F32
        ).reshape(count, width)
        mixed_rows[...] = mixed + own_prob * own_value
        for g in range(per_kv):
            piece = mixed_rows[pl.ds(g, part, stride=per_kv), :].astype(BF16)
            att[j, me, :, g * width:(g + 1) * width] = piece
            own_att[h * part:(h + 1) * part, k * feats + g * width:k * feats + (g + 1) * width] = piece
        if j == 0:
            get_a.start()
            for get in get_w:
                get.start()
            get_up.start()
        if j == GREETED:
            pl.semaphore_wait(barrier, n - 1 + nt - 1)
            for i in range(1, n):
                pos_copy(i).start()
            for i in range(j):
                pass_on(i, 0, lambda copy: copy.start())
        if j >= GREETED:
            pass_on(j, 0, lambda copy: copy.start())

    def base(i):
        get_w[i].wait()
        partial = jnp.dot(own_att[...], w[i], preferred_element_type=F32)
        if i < nt - 1:
            base_send[i] = partial.astype(BF16)
            base_copy(i).start()
        else:
            base_own[...] = partial

    every = n * part
    short = every // 2
    packs = LANES // rank
    half = iota((every, LANES), 1) // rank
    low = iota((short, LANES), 1) < rank

    def keeps(h, j):
        where = positions[:, h * part:(h + 1) * part, :].reshape(every, LANES) - (me * stored).astype(F32)
        return where == (half + j * packs).astype(F32)

    def shrink(h):
        if h == 0:
            get_a.wait()
            for i in range(1, n):
                pos_copy(i).wait_recv()
        down = jnp.zeros((every, stored * rank), F32)
        for k in range(kv):
            down = down + lax.dot_general(
                att[h * kv + k].reshape(every, feats), a[:, k * feats:(k + 1) * feats],
                (((1,), (1,)), ((), ())), preferred_element_type=F32,
            )
        folded = jnp.zeros((every, LANES), F32)
        for j in range(stored // packs):
            folded = folded + jnp.where(keeps(h, j), down[:, j * LANES:(j + 1) * LANES], 0.0)
        folded = folded + pltpu.roll(folded, rank, 1)
        shrunk[h, 0] = jnp.where(low, folded[:short], folded[short:]).astype(BF16)
        for i in range(1, nt):
            shrink_copy(h, i).start()

    def expand(h):
        if h == 0:
            get_up.wait()
        total = shrunk[h, 0].astype(F32)
        for i in range(1, nt):
            shrink_copy(h, i).wait_recv()
            total = total + shrunk[h, i].astype(F32)
        turned = pltpu.roll(total, rank, 1)
        whole = jnp.concatenate([jnp.where(low, total, turned), jnp.where(low, turned, total)], axis=0)
        spread = jnp.concatenate(
            [jnp.where(keeps(h, j), whole, 0.0) for j in range(stored // packs)], axis=1
        ).astype(BF16)
        delta = jnp.dot(spread, up[...], preferred_element_type=F32) * ADAPTER_SCALING
        delta_send[h] = delta.astype(BF16).reshape(n, part, out_share)
        for i in range(1, n):
            delta_copy(h, i).start()

    events = sorted(
        ((j, d) for j in range(len(chunks)) for d in range(1, n)),
        key=lambda e: (e[0] + 3 * ((e[1] - 1) // stride(e[0])), -e[1]),
    )
    bases = list(range(nt))
    last = {h: max(i for i, (j, d) in enumerate(events) if chunks[j][0] == h) for h in range(HALVES)}
    for at, (j, d) in enumerate(events):
        handed = d % stride(j) == 0 and d < n - 1
        if not handed:
            while len(bases) > 1 and not any(e[1] % stride(e[0]) == 0 and e[1] < n - 1 for e in events[at:]):
                base(bases.pop(0))
        arrive(j, d)
        if handed and len(bases) > 1:
            base(bases.pop(0))
        for h in range(HALVES):
            if last[h] == at:
                shrink(h)
    for i in bases:
        base(i)
    for h in range(HALVES):
        expand(h)

    for h in range(HALVES):
        here = slice(h * part, (h + 1) * part)
        result = base_own[here] + delta_send[h, me].astype(F32)
        for i in range(nt - 1):
            if h == 0:
                base_copy(i).wait_recv()
            result = result + base_recv[i, here].astype(F32)
        for i in range(1, n):
            delta_copy(h, i).wait_recv()
            result = result + delta_recv[h, i - 1].astype(F32)
        out_ref[here] = result.astype(BF16)

    for i in range(1, n):
        pos_copy(i).wait_send()
        for h in range(HALVES):
            delta_copy(h, i).wait_send()
    for i in range(1, nt):
        for h in range(HALVES):
            shrink_copy(h, i).wait_send()
    for i in range(nt - 1):
        base_copy(i).wait_send()
    for j in range(len(chunks)):
        for source in range(0, n, stride(j)):
            pass_on(j, source, lambda copy: copy.wait_send())


def local(
    n, nt,
    queries, cache_keys, cache_values, new_key, new_value, lengths,
    adapter_ids, adapter_home, w_out, factor_a, up_factor_table,
):
    rows, heads, width = queries.shape
    kv, span = cache_keys.shape[1:3]
    stored, rank, feats_all = factor_a.shape
    out_share = up_factor_table.shape[2]
    feats = feats_all // kv
    per_kv = heads // kv
    dma = pltpu.SemaphoreType.DMA
    vmem = pl.BlockSpec(memory_space=pltpu.VMEM)
    hbm = pl.BlockSpec(memory_space=pltpu.HBM)
    chunks = HALVES * kv
    part = rows // HALVES
    return pl.pallas_call(
        functools.partial(kernel, n, nt, rank),
        out_shape=jax.ShapeDtypeStruct((rows, out_share), BF16),
        in_specs=[hbm] * 11,
        out_specs=vmem,
        scratch_shapes=[
            pltpu.VMEM((1, rows), jnp.int32),
            pltpu.VMEM((1, rows), jnp.int32),
            pltpu.VMEM((1, adapter_home.shape[0]), jnp.int32),
            pltpu.VMEM((rows * kv, width), BF16),
            pltpu.VMEM((rows * kv, width), BF16),
            pltpu.VMEM((rows, heads, width), BF16),
            pltpu.VMEM((kv, rows, span, width), BF16),
            pltpu.VMEM((kv, rows, span, width), BF16),
            pltpu.VMEM((nt, feats_all, out_share), BF16),
            pltpu.VMEM((stored * rank, feats_all), BF16),
            pltpu.VMEM((stored * rank, out_share), BF16),
            pltpu.VMEM((part * per_kv, width), F32),
            pltpu.VMEM((rows, feats_all), BF16),
            pltpu.VMEM((chunks, n, part, feats), BF16),
            pltpu.VMEM((n, rows, LANES), F32),
            pltpu.VMEM((HALVES, nt, n * part // 2, LANES), BF16),
            pltpu.VMEM((nt - 1, rows, out_share), BF16),
            pltpu.VMEM((nt - 1, rows, out_share), BF16),
            pltpu.VMEM((rows, out_share), F32),
            pltpu.VMEM((HALVES, n, part, out_share), BF16),
            pltpu.VMEM((HALVES, n - 1, part, out_share), BF16),
            dma((5,)), dma, dma((chunks,)), dma((chunks,)), dma((nt,)), dma, dma,
            dma((n,)), dma((n,)),
            dma((chunks, n)), dma((chunks, n)), dma((chunks, n)), dma((chunks, n)),
            dma((HALVES, nt)), dma((HALVES, nt)),
            dma((nt,)), dma((nt,)),
            dma((HALVES, n)), dma((HALVES, n)),
        ],
        compiler_params=pltpu.CompilerParams(
            collective_id=0, has_side_effects=True, vmem_limit_bytes=60 * 1024 * 1024
        ),
        name="attend_project",
    )(
        lengths, adapter_ids.reshape(1, rows), adapter_home.reshape(1, -1),
        new_key.reshape(rows * kv, width), new_value.reshape(rows * kv, width),
        queries, cache_keys, cache_values, w_out,
        factor_a.reshape(stored * rank, feats_all), up_factor_table.reshape(stored * rank, out_share),
    )


def solution(mesh):
    in_specs = (
        P(("parts", "dp"), "tensor", None),
        P(("parts", "dp"), "tensor", None, None),
        P(("parts", "dp"), "tensor", None, None),
        P(("parts", "dp"), "tensor", None),
        P(("parts", "dp"), "tensor", None),
        P(("parts", "dp"), None),
        P(("parts", "dp")),
        P("parts"),
        P("tensor", None),
        P("dp", None, "tensor"),
        P("dp", None, "tensor"),
    )
    out_specs = P(("parts", "dp"), "tensor")
    body = functools.partial(local, mesh.shape["dp"], mesh.shape["tensor"])
    return jax.shard_map(body, mesh=mesh, in_specs=in_specs, out_specs=out_specs, check_vma=False)
```

```python
import functools
import math

import jax
import jax.numpy as jnp
from jax import lax
from jax.experimental import pallas as pl
from jax.experimental.pallas import tpu as pltpu
from jax.sharding import PartitionSpec as P

ADAPTER_SCALING = 2.0
MESH = pl.DeviceIdType.MESH
F32 = jnp.float32
BF16 = jnp.bfloat16
LANES = 128
HALVES = 1
STRIDES = (1, 1)


def iota(shape, dim):
    return lax.broadcasted_iota(jnp.int32, shape, dim)


def stride(j):
    return STRIDES[min(j, len(STRIDES) - 1)]


def column(row, count, spread):
    shape = (count * spread, count)
    own = iota(shape, 0) // spread == iota(shape, 1)
    return jnp.sum(jnp.where(own, row.astype(F32), 0.0), axis=1, keepdims=True)


def kernel(
    n, nt, rank,
    lengths_hbm, ids_hbm, home_hbm, new_key_hbm, new_value_hbm,
    queries_hbm, keys_hbm, values_hbm, w_hbm, a_hbm, up_hbm,
    out_ref,
    lengths, ids, home, new_key, new_value,
    queries, keys, values, w, a, up,
    mixed_rows, own_att, att, positions, shrunk, base_send, base_recv, base_own, delta_send, delta_recv,
    load_small, load_q, load_k, load_v, load_w, load_a, load_up,
    right_send, right_recv, left_send, left_recv,
    shrink_send, shrink_recv, bsend, brecv, dsend, drecv,
):
    rows, heads, width = queries.shape
    kv, span = keys.shape[0], keys.shape[2]
    per_kv = heads // kv
    feats = per_kv * width
    out_share = up.shape[1]
    stored = up.shape[0] // rank
    part = rows // HALVES
    me = lax.axis_index("dp")
    mt = lax.axis_index("tensor")

    def block(t):
        return pl.ds(pl.multiple_of(t * out_share, out_share), out_share)

    small = [(ids_hbm, ids), (home_hbm, home), (lengths_hbm, lengths), (new_key_hbm, new_key), (new_value_hbm, new_value)]
    get_small = [pltpu.make_async_copy(x, y, load_small.at[i]) for i, (x, y) in enumerate(small)]
    for get in get_small:
        get.start()
    get_q = pltpu.make_async_copy(queries_hbm, queries, load_q)
    get_q.start()
    chunks = [(h, k) for h in range(HALVES) for k in range(kv)]
    get_k, get_v = [], []
    for j, (h, k) in enumerate(chunks):
        here = pl.ds(h * part, part)
        get_k.append(pltpu.make_async_copy(keys_hbm.at[here, k], keys.at[k, here], load_k.at[j]))
        get_v.append(pltpu.make_async_copy(values_hbm.at[here, k], values.at[k, here], load_v.at[j]))
        if j == 0:
            get_k[j].start()
            get_v[j].start()
    get_w = []
    for i in range(nt):
        t = lax.rem(mt + 1 + i, nt)
        get_w.append(pltpu.make_async_copy(w_hbm.at[:, block(t)], w.at[i], load_w.at[i]))
    get_a = pltpu.make_async_copy(a_hbm, a, load_a)
    get_up = pltpu.make_async_copy(up_hbm, up, load_up)

    barrier = pltpu.get_barrier_semaphore()
    for i in range(1, n):
        pl.semaphore_signal(barrier, inc=1, device_id={"dp": lax.rem(me + i, n)}, device_id_type=MESH)
    for i in range(1, nt):
        pl.semaphore_signal(barrier, inc=1, device_id={"tensor": lax.rem(mt + i, nt)}, device_id_type=MESH)

    for get in get_small:
        get.wait()
    def line(j, slot, distance, step, sign):
        send, recv = (right_send, right_recv) if sign > 0 else (left_send, left_recv)
        piece = positions.at[slot] if j == len(chunks) else att.at[j, slot]
        return pltpu.make_async_remote_copy(
            src_ref=piece, dst_ref=piece,
            send_sem=send.at[j, distance], recv_sem=recv.at[j, distance],
            device_id={"dp": me + sign * step}, device_id_type=MESH,
        )

    def reaches(offset):
        return (me + offset >= 0) & (me + offset <= n - 1)

    def pass_on(j, source, act):
        for step in range(min(stride(j), n - 1), 0, -1):
            for sign in (1, -1):
                if source + step < n:
                    @pl.when(reaches(sign * step) & reaches(-sign * source))
                    def _():
                        act(line(j, me - sign * source, source + step, step, sign))

    def arrive(j, distance):
        for sign in (1, -1):
            @pl.when(reaches(-sign * distance))
            def _():
                came = (distance - 1) % stride(j) + 1
                line(j, me - sign * distance, distance, came, sign).wait_recv()
        if distance % stride(j) == 0:
            pass_on(j, distance, lambda copy: copy.start())

    def base_copy(i):
        return pltpu.make_async_remote_copy(
            src_ref=base_send.at[i], dst_ref=base_recv.at[i],
            send_sem=bsend.at[i], recv_sem=brecv.at[i],
            device_id={"tensor": lax.rem(mt + 1 + i, nt)}, device_id_type=MESH,
        )

    def shrink_copy(h, i):
        return pltpu.make_async_remote_copy(
            src_ref=shrunk.at[h, 0], dst_ref=shrunk.at[h, i],
            send_sem=shrink_send.at[h, i], recv_sem=shrink_recv.at[h, i],
            device_id={"tensor": lax.rem(mt + i, nt)}, device_id_type=MESH,
        )

    def delta_copy(h, i):
        to = lax.rem(me + i, n)
        return pltpu.make_async_remote_copy(
            src_ref=delta_send.at[h, to], dst_ref=delta_recv.at[h, i - 1],
            send_sem=dsend.at[h, i - 1], recv_sem=drecv.at[h, i - 1],
            device_id={"dp": to}, device_id_type=MESH,
        )

    count = part * per_kv
    scale = 1.0 / math.sqrt(width)
    reach = column(lengths[...], rows, per_kv)
    get_q.wait()
    for j, (h, k) in enumerate(chunks):
        visible = iota((count, span), 1).astype(F32) < reach[h * count:(h + 1) * count]
        q = queries[h * part:(h + 1) * part]
        get_k[j].wait()
        if j + 1 < len(chunks):
            get_k[j + 1].start()
            get_v[j + 1].start()
        scores = lax.dot_general(
            q, keys[k, h * part:(h + 1) * part], (((2,), (2,)), ((0,), (0,))), preferred_element_type=F32
        )[:, k * per_kv:(k + 1) * per_kv, :].reshape(count, span) * scale
        row = iota((count, rows * kv), 0) // per_kv + h * part
        pick = (iota((count, rows * kv), 1) == row * kv + k).astype(BF16)
        own_key = jnp.dot(pick, new_key[...], preferred_element_type=F32)
        own_value = jnp.dot(pick, new_value[...], preferred_element_type=F32)
        qk = q.astype(F32)[:, k * per_kv:(k + 1) * per_kv, :].reshape(count, width)
        own = jnp.sum(qk * own_key, axis=1, keepdims=True) * scale
        top = jnp.maximum(jnp.max(jnp.where(visible, scores, -jnp.inf), axis=1, keepdims=True), own)
        weights = jnp.where(visible, jnp.exp(scores - top), 0.0)
        own_weight = jnp.exp(own - top)
        total = jnp.sum(weights, axis=1, keepdims=True) + own_weight
        probs = (weights / total).reshape(part, per_kv, span).astype(BF16)
        own_prob = (own_weight / total).astype(BF16).astype(F32)
        get_v[j].wait()
        mixed = lax.dot_general(
            probs, values[k, h * part:(h + 1) * part], (((2,), (1,)), ((0,), (0,))), preferred_element_type=F32
        ).reshape(count, width)
        mixed_rows[...] = mixed + own_prob * own_value
        for g in range(per_kv):
            piece = mixed_rows[pl.ds(g, part, stride=per_kv), :].astype(BF16)
            att[j, me, :, g * width:(g + 1) * width] = piece
            own_att[h * part:(h + 1) * part, k * feats + g * width:k * feats + (g + 1) * width] = piece
        if j == 0:
            get_a.start()
            for get in get_w:
                get.start()
            get_up.start()
            pl.semaphore_wait(barrier, n - 1 + nt - 1)
        pass_on(j, 0, lambda copy: copy.start())
        if j == 0:
            adapters = home.shape[1]
            id_column = column(ids[...], rows, 1)
            match = id_column == iota((rows, adapters), 1).astype(F32)
            position = jnp.sum(jnp.where(match, home[...].astype(F32), 0.0), axis=1, keepdims=True)
            positions[me] = jnp.broadcast_to(position, (rows, LANES))
            pass_on(len(chunks), 0, lambda copy: copy.start())

    def base(i):
        get_w[i].wait()
        partial = jnp.dot(own_att[...], w[i], preferred_element_type=F32)
        if i < nt - 1:
            base_send[i] = partial.astype(BF16)
            base_copy(i).start()
        else:
            base_own[...] = partial

    every = n * part
    short = every // 2
    packs = LANES // rank
    half = iota((every, LANES), 1) // rank
    low = iota((short, LANES), 1) < rank

    def keeps(h, j):
        where = positions[:, h * part:(h + 1) * part, :].reshape(every, LANES) - (me * stored).astype(F32)
        return where == (half + j * packs).astype(F32)

    def shrink(h):
        if h == 0:
            get_a.wait()
        down = jnp.zeros((every, stored * rank), F32)
        for k in range(kv):
            down = down + lax.dot_general(
                att[h * kv + k].reshape(every, feats), a[:, k * feats:(k + 1) * feats],
                (((1,), (1,)), ((), ())), preferred_element_type=F32,
            )
        folded = jnp.zeros((every, LANES), F32)
        for j in range(stored // packs):
            folded = folded + jnp.where(keeps(h, j), down[:, j * LANES:(j + 1) * LANES], 0.0)
        folded = folded + pltpu.roll(folded, rank, 1)
        shrunk[h, 0] = jnp.where(low, folded[:short], folded[short:]).astype(BF16)
        for i in range(1, nt):
            shrink_copy(h, i).start()

    def expand(h):
        if h == 0:
            get_up.wait()
        total = shrunk[h, 0].astype(F32)
        for i in range(1, nt):
            shrink_copy(h, i).wait_recv()
            total = total + shrunk[h, i].astype(F32)
        turned = pltpu.roll(total, rank, 1)
        whole = jnp.concatenate([jnp.where(low, total, turned), jnp.where(low, turned, total)], axis=0)
        spread = jnp.concatenate(
            [jnp.where(keeps(h, j), whole, 0.0) for j in range(stored // packs)], axis=1
        ).astype(BF16)
        delta = jnp.dot(spread, up[...], preferred_element_type=F32) * ADAPTER_SCALING
        delta_send[h] = delta.astype(BF16).reshape(n, part, out_share)
        for i in sorted(range(1, n), key=lambda i: min(i, n - i)):
            delta_copy(h, i).start()

    events = sorted(
        ((j, d) for j in range(len(chunks) + 1) for d in range(1, n)),
        key=lambda e: ((e[0] if e[0] < len(chunks) else 0.5) + 3 * ((e[1] - 1) // stride(e[0])), -e[1]),
    )
    bases = list(range(nt))
    last = {h: max(i for i, (j, d) in enumerate(events) if j < len(chunks) and chunks[j][0] == h) for h in range(HALVES)}
    for at, (j, d) in enumerate(events):
        handed = d % stride(j) == 0 and d < n - 1
        if not handed:
            while len(bases) > 1 and not any(e[1] % stride(e[0]) == 0 and e[1] < n - 1 for e in events[at:]):
                base(bases.pop(0))
        arrive(j, d)
        if handed and j < len(chunks) and len(bases) > 1:
            base(bases.pop(0))
        for h in range(HALVES):
            if last[h] == at:
                shrink(h)
    for i in bases:
        base(i)
    for h in range(HALVES):
        expand(h)

    for h in range(HALVES):
        here = slice(h * part, (h + 1) * part)
        result = base_own[here] + delta_send[h, me].astype(F32)
        for i in range(nt - 1):
            if h == 0:
                base_copy(i).wait_recv()
            result = result + base_recv[i, here].astype(F32)
        for i in range(1, n):
            delta_copy(h, i).wait_recv()
            result = result + delta_recv[h, i - 1].astype(F32)
        out_ref[here] = result.astype(BF16)

    for i in range(1, n):
        for h in range(HALVES):
            delta_copy(h, i).wait_send()
    for i in range(1, nt):
        for h in range(HALVES):
            shrink_copy(h, i).wait_send()
    for i in range(nt - 1):
        base_copy(i).wait_send()
    for j in range(len(chunks) + 1):
        for source in range(0, n, stride(j)):
            pass_on(j, source, lambda copy: copy.wait_send())


def local(
    n, nt,
    queries, cache_keys, cache_values, new_key, new_value, lengths,
    adapter_ids, adapter_home, w_out, factor_a, up_factor_table,
):
    rows, heads, width = queries.shape
    kv, span = cache_keys.shape[1:3]
    stored, rank, feats_all = factor_a.shape
    out_share = up_factor_table.shape[2]
    feats = feats_all // kv
    per_kv = heads // kv
    dma = pltpu.SemaphoreType.DMA
    vmem = pl.BlockSpec(memory_space=pltpu.VMEM)
    hbm = pl.BlockSpec(memory_space=pltpu.HBM)
    chunks = HALVES * kv
    part = rows // HALVES
    return pl.pallas_call(
        functools.partial(kernel, n, nt, rank),
        out_shape=jax.ShapeDtypeStruct((rows, out_share), BF16),
        in_specs=[hbm] * 11,
        out_specs=vmem,
        scratch_shapes=[
            pltpu.VMEM((1, rows), jnp.int32),
            pltpu.VMEM((1, rows), jnp.int32),
            pltpu.VMEM((1, adapter_home.shape[0]), jnp.int32),
            pltpu.VMEM((rows * kv, width), BF16),
            pltpu.VMEM((rows * kv, width), BF16),
            pltpu.VMEM((rows, heads, width), BF16),
            pltpu.VMEM((kv, rows, span, width), BF16),
            pltpu.VMEM((kv, rows, span, width), BF16),
            pltpu.VMEM((nt, feats_all, out_share), BF16),
            pltpu.VMEM((stored * rank, feats_all), BF16),
            pltpu.VMEM((stored * rank, out_share), BF16),
            pltpu.VMEM((part * per_kv, width), F32),
            pltpu.VMEM((rows, feats_all), BF16),
            pltpu.VMEM((chunks, n, part, feats), BF16),
            pltpu.VMEM((n, rows, LANES), F32),
            pltpu.VMEM((HALVES, nt, n * part // 2, LANES), BF16),
            pltpu.VMEM((nt - 1, rows, out_share), BF16),
            pltpu.VMEM((nt - 1, rows, out_share), BF16),
            pltpu.VMEM((rows, out_share), F32),
            pltpu.VMEM((HALVES, n, part, out_share), BF16),
            pltpu.VMEM((HALVES, n - 1, part, out_share), BF16),
            dma((5,)), dma, dma((chunks,)), dma((chunks,)), dma((nt,)), dma, dma,
            dma((chunks + 1, n)), dma((chunks + 1, n)), dma((chunks + 1, n)), dma((chunks + 1, n)),
            dma((HALVES, nt)), dma((HALVES, nt)),
            dma((nt,)), dma((nt,)),
            dma((HALVES, n)), dma((HALVES, n)),
        ],
        compiler_params=pltpu.CompilerParams(
            collective_id=0, has_side_effects=True, vmem_limit_bytes=60 * 1024 * 1024
        ),
        name="attend_project",
    )(
        lengths, adapter_ids.reshape(1, rows), adapter_home.reshape(1, -1),
        new_key.reshape(rows * kv, width), new_value.reshape(rows * kv, width),
        queries, cache_keys, cache_values, w_out,
        factor_a.reshape(stored * rank, feats_all), up_factor_table.reshape(stored * rank, out_share),
    )


def solution(mesh):
    in_specs = (
        P(("parts", "dp"), "tensor", None),
        P(("parts", "dp"), "tensor", None, None),
        P(("parts", "dp"), "tensor", None, None),
        P(("parts", "dp"), "tensor", None),
        P(("parts", "dp"), "tensor", None),
        P(("parts", "dp"), None),
        P(("parts", "dp")),
        P("parts"),
        P("tensor", None),
        P("dp", None, "tensor"),
        P("dp", None, "tensor"),
    )
    out_specs = P(("parts", "dp"), "tensor")
    body = functools.partial(local, mesh.shape["dp"], mesh.shape["tensor"])
    return jax.shard_map(body, mesh=mesh, in_specs=in_specs, out_specs=out_specs, check_vma=False)
```
